512 devices in a mesh: seq: 128 (over z_lo, x, y, core), chan: 4 (over z_hi).
Axes of the slice: x: 4, y: 4, z: 16 (z_hi: 4, z_lo: 4; z = z_hi * 4 + z_lo), core: 2. Of those that a mesh axis runs over, the one named last changes fastest.
Arguments:
- inputs: bfloat16 [16384, 4096], P('seq'), may hold values from -24 to 24
- proj_weight: bfloat16 [3, 256, 4096], P(None, 'chan'), may hold values from -0.09375 to 0.09375
- filters: float32 [16384, 256], P('seq', 'chan'), may hold values from -2 to 2
- out_grad: bfloat16 [16384, 256], P('seq', 'chan'), may hold values from -6 to 6
Outputs:
- gated: bfloat16 [16384, 256], P('seq', 'chan')
- weight_grad: bfloat16 [4096, 3, 256], P('seq', None, 'chan')
- input_grad: bfloat16 [16384, 4096], P('seq', 'chan')
The draws below stay inside these ranges and needn't reach their ends.
All inputs are finite; a program needn't handle non-finite values.
Results may differ from the reference program's by a relative error of at most 0.023.
Values may be sent and summed in bfloat16 or wider, within the bound.
No kernel may reach another device: no remote copies, remote signals or barrier semaphores. Data moves between devices by JAX's collectives and lax.ppermute only.
A program may use at most 64 MiB of HBM per device.

```python
import math
import jax
import jax.numpy as jnp
from jax import lax

D = 4096
CH_DEV = 64
LENGTH = 16384
CHANNELS = 256
N_CHAN = 4


def draw_filters(key, part):
    key = jax.random.fold_in(key, 7)
    key_rough, key_rate, key_place = jax.random.split(key, 3)
    low_rate = math.log(0.5 / LENGTH)
    high_rate = math.log(1.0 / 30.0)
    rough = jax.random.normal(key_rough, (LENGTH, CHANNELS), jnp.float32)
    rates = jnp.exp(jax.random.uniform(key_rate, (1, CHANNELS), jnp.float32, low_rate, high_rate))
    places = jax.random.randint(key_place, (3,), 0, LENGTH)
    steps_int = jnp.arange(LENGTH, dtype=jnp.int32)
    drops = jnp.sum((steps_int[:, None] >= places[None, :]).astype(jnp.float32), axis=1, keepdims=True)
    taps = steps_int.astype(jnp.float32)[:, None]
    envelope = jnp.exp(-rates * taps) * jnp.power(0.6, drops)
    norm = jnp.sqrt(2.0 * rates / (1.0 - jnp.exp(-2.0 * rates * LENGTH)))
    return (rough * envelope * norm).astype(jnp.float32)


def raised(entries, rng, source, target, blocks, factor):
    owner, partner = [(jnp.arange(entries.shape[position]) // (entries.shape[position] // blocks)).reshape([-1 if axis == position else 1 for axis in range(entries.ndim)]) for position in (source, target)]
    chosen = jax.random.permutation(rng, blocks)[partner]
    strong = (owner == chosen) | (owner == (partner + blocks // 2) % blocks)
    return jnp.where(strong, factor * entries, entries)


def steps_of(own_key, shape, shards, least, high):
    factor_of, own = 1.0, jax.random.fold_in(own_key, 6)
    for axis_at, shards_of in shards:
        heights = jnp.exp(jax.random.uniform(jax.random.fold_in(own, axis_at), (shards_of,), jnp.float32, least / len(shards), high / len(shards)))
        factor_of = factor_of * jnp.repeat(heights, shape[axis_at] // shards_of).reshape([-1 if axis == axis_at else 1 for axis in range(len(shape))])
    return factor_of


def bell_draw(rng, extent, width, limit, pieces=(), kind=jnp.bfloat16):
    values = width * jax.random.normal(rng, extent, jnp.float32)
    if pieces:
        values = values * steps_of(rng, extent, pieces, -0.22, 0.18)
    return jnp.clip(values, -limit, limit).astype(kind)


def heavy_noise(stream_key, shape, width, reach, cuts, heavy, kind=jnp.bfloat16):
    entries = width * jax.random.normal(stream_key, shape, jnp.float32)
    if cuts:
        entries = entries * steps_of(stream_key, shape, cuts, -0.22, 0.18)
    return jnp.clip(raised(entries, jax.random.fold_in(stream_key, 3), *heavy), -reach, reach).astype(kind)


def setup_inputs(seed: int = 0) -> dict:
    arg_keys = jax.random.split(jax.random.key(seed), 5)
    return {
        "inputs": heavy_noise(arg_keys[0], (LENGTH, D), 1.0, 24.0, ((0, 128),), (0, 1, 128, 5.5)),
        "proj_weight": bell_draw(arg_keys[1], (3, CHANNELS, D), D ** -0.5, 0.09375, ((1, 4),)),
        "filters": draw_filters(jax.random.fold_in(arg_keys[4], 71), 0),
        "out_grad": bell_draw(arg_keys[3], (LENGTH, CHANNELS), 1.0, 6.0, ((0, 128), (1, 4))),
    }


def reference(inputs, proj_weight, filters, out_grad):
    f32 = jnp.float32
    bf16 = jnp.bfloat16
    flat_w = proj_weight.reshape(3 * CHANNELS, D)
    fields = lax.dot_general(inputs, flat_w, (((1,), (1,)), ((), ())), preferred_element_type=f32).astype(bf16)
    query = fields[:, :CHANNELS].astype(f32)
    keys = fields[:, CHANNELS:2 * CHANNELS].astype(f32)
    values = fields[:, 2 * CHANNELS:].astype(f32)
    mixed = keys * values
    total = 2 * LENGTH
    spec_filter = jnp.fft.rfft(filters, n=total, axis=0)
    conv = jnp.fft.irfft(jnp.fft.rfft(mixed, n=total, axis=0) * spec_filter, n=total, axis=0)[:LENGTH]
    gated = (query * conv).astype(bf16)
    grad = out_grad.astype(f32)
    grad_query = (grad * conv).astype(bf16)
    grad_conv = grad * query
    grad_mixed = jnp.fft.irfft(jnp.fft.rfft(grad_conv, n=total, axis=0) * jnp.conj(spec_filter), n=total, axis=0)[:LENGTH]
    grad_key = (grad_mixed * values).astype(bf16)
    grad_value = (grad_mixed * keys).astype(bf16)
    grads = jnp.concatenate([grad_query, grad_key, grad_value], axis=1)
    scale = 1.0 / math.sqrt(LENGTH)
    summed = jnp.dot(inputs.T, grads, preferred_element_type=f32) * scale
    weight_grad = summed.reshape(D, 3, CHANNELS).astype(bf16)
    accum = jnp.zeros((LENGTH, D), f32)
    for group in range(N_CHAN):
        low = group * CH_DEV
        high = low + CH_DEV
        group_grads = jnp.concatenate([grad_query[:, low:high], grad_key[:, low:high], grad_value[:, low:high]], axis=1)
        group_w = proj_weight[:, low:high, :].reshape(3 * CH_DEV, D)
        partial_sum = jnp.dot(group_grads, group_w, preferred_element_type=f32)
        accum = accum + lax.optimization_barrier(partial_sum.astype(bf16)).astype(f32)
    input_grad = accum.astype(bf16)
    return (gated, weight_grad, input_grad)
```

```python
import math

import jax
import jax.numpy as jnp
import numpy as np
from jax import lax
from jax.experimental import pallas as pl
from jax.experimental.pallas import tpu as pltpu
from jax.sharding import Mesh, PartitionSpec as P

F32 = jnp.float32
BF16 = jnp.bfloat16
SEQ = ("z", "x", "y", "core")
ROWS = 128
CH = 64
VMEM_LIMIT = 48 * 1024 * 1024


def params(*semantics):
    return pltpu.CompilerParams(
        vmem_limit_bytes=VMEM_LIMIT, dimension_semantics=semantics or None
    )


def nt_dot(left, right):
    return lax.dot_general(left, right, (((1,), (1,)), ((), ())), preferred_element_type=F32)


def tn_dot(left, right):
    return lax.dot_general(left, right, (((0,), (0,)), ((), ())), preferred_element_type=F32)


def nn_dot(left, right):
    return jnp.dot(left, right, preferred_element_type=F32)


def tables():
    length = ROWS * ROWS
    index = np.arange(ROWS)
    first = np.exp(-2j * np.pi * np.outer(index + 0.25, index) / ROWS)
    twist = np.exp(-2j * np.pi * np.outer(index + 0.25, index) / length)
    second = np.exp(-2j * np.pi * np.outer(index, index) / ROWS)
    first_rows = np.concatenate([first.real, first.imag], axis=0)
    second_fwd = np.block([[second.real, second.imag], [-second.imag, second.real]])
    second_bwd = np.block([[second.real, -second.imag], [second.imag, second.real]])
    first_bwd = np.concatenate([first.real.T, first.imag.T], axis=1) / length
    as_bf16 = lambda x: jnp.asarray(x, dtype=BF16)
    as_f32 = lambda x: jnp.asarray(x, dtype=F32)
    return (
        as_bf16(first_rows),
        as_f32(twist.real),
        as_f32(twist.imag),
        as_bf16(second_fwd),
        as_bf16(second_bwd),
        as_bf16(first_bwd),
    )


def fields_kernel(x_ref, w_ref, filt_ref, grad_ref, fields_ref, send_ref, acc, scratch):
    step = pl.program_id(0)

    @pl.when(step == 0)
    def _():
        acc[...] = jnp.zeros_like(acc)

    acc[...] += nt_dot(w_ref[...], x_ref[...])

    @pl.when(step == pl.num_programs(0) - 1)
    def _():
        fields = acc[...].astype(BF16)
        fields_ref[0 : 3 * CH, :] = fields
        grad_t = grad_ref[...].astype(F32).T
        fields_ref[3 * CH : 4 * CH, :] = grad_t.astype(BF16)
        query = fields[0:CH].astype(F32)
        key = fields[CH : 2 * CH].astype(F32)
        value = fields[2 * CH : 3 * CH].astype(F32)
        filt_t = filt_ref[...].T
        scratch[pl.ds(0, CH, stride=4), :] = key * value
        scratch[pl.ds(1, CH, stride=4), :] = filt_t
        scratch[pl.ds(2, CH, stride=4), :] = grad_t * query
        scratch[pl.ds(3, CH, stride=4), :] = filt_t
        send_ref[...] = scratch[...].astype(BF16)


def fields_call(inputs, flat_w, filters, out_grad):
    width = inputs.shape[1]
    tile = 1024
    return pl.pallas_call(
        fields_kernel,
        grid=(width // tile,),
        in_specs=[
            pl.BlockSpec((ROWS, tile), lambda i: (0, i)),
            pl.BlockSpec((3 * CH, tile), lambda i: (0, i)),
            pl.BlockSpec((ROWS, CH), lambda i: (0, 0)),
            pl.BlockSpec((ROWS, CH), lambda i: (0, 0)),
        ],
        out_specs=[
            pl.BlockSpec((4 * CH, ROWS), lambda i: (0, 0)),
            pl.BlockSpec((4 * CH, ROWS), lambda i: (0, 0)),
        ],
        out_shape=[
            jax.ShapeDtypeStruct((4 * CH, ROWS), BF16),
            jax.ShapeDtypeStruct((4 * CH, ROWS), BF16),
        ],
        scratch_shapes=[
            pltpu.VMEM((3 * CH, ROWS), F32),
            pltpu.VMEM((4 * CH, ROWS), F32),
        ],
        compiler_params=params("arbitrary"),
        name="fields",
    )(inputs, flat_w, filters, out_grad)


def flip_kernel(x_ref, out_ref):
    step = pl.program_id(0)
    for x_y in range(16):
        block = x_ref[:, 64 * x_y : 64 * (x_y + 1)].astype(F32).T.astype(BF16)
        for core in range(2):
            out_ref[core, x_y, :, :] = block[32 * core : 32 * (core + 1), :]


def flip_call(inputs):
    out = pl.pallas_call(
        flip_kernel,
        grid=(4,),
        in_specs=[pl.BlockSpec((ROWS, 1024), lambda i: (0, i))],
        out_specs=pl.BlockSpec((2, 16, 32, ROWS), lambda i: (0, 0, i, 0)),
        out_shape=jax.ShapeDtypeStruct((2, 16, 128, ROWS), BF16),
        compiler_params=params("arbitrary"),
        name="flip",
    )(inputs)
    return out.reshape(4096, ROWS)


def conv_kernel(got_ref, e1_ref, twr_ref, twi_ref, e2_ref, e2b_ref, e1b_ref, out_ref, scratch):
    sign = jnp.where(lax.axis_index("core") == 0, 1.0, -1.0).astype(F32)
    scratch[...] = got_ref[...].astype(F32)
    signal = scratch[pl.ds(0, ROWS, stride=2), :].astype(BF16)
    filt = scratch[pl.ds(1, ROWS, stride=2), :].astype(BF16)
    twr, twi = twr_ref[...], twi_ref[...]

    both = nn_dot(e1_ref[...], jnp.concatenate([signal, filt], axis=1))

    def twisted(part):
        re, im = part[0:ROWS], part[ROWS:]
        return jnp.concatenate([re * twr - im * twi, re * twi + im * twr], axis=1)

    mid = jnp.concatenate([twisted(both[:, 0:ROWS]), twisted(both[:, ROWS:])], axis=0)
    spec = nn_dot(mid.astype(BF16), e2_ref[...])
    sig_re, sig_im = spec[0:ROWS, 0:ROWS], spec[0:ROWS, ROWS:]
    fil_re, fil_im = spec[ROWS:, 0:ROWS], spec[ROWS:, ROWS:] * sign
    prod_re = sig_re * fil_re - sig_im * fil_im
    prod_im = sig_re * fil_im + sig_im * fil_re
    prod = jnp.concatenate([prod_re, prod_im], axis=1).astype(BF16)
    back = nn_dot(prod, e2b_ref[...])
    re, im = back[:, 0:ROWS], back[:, ROWS:]
    stack = jnp.concatenate([re * twr + im * twi, im * twr - re * twi], axis=0).astype(BF16)
    out_ref[...] = nn_dot(e1b_ref[...], stack)


def conv_call(got):
    return pl.pallas_call(
        conv_kernel,
        out_shape=jax.ShapeDtypeStruct((ROWS, ROWS), F32),
        scratch_shapes=[pltpu.VMEM((2 * ROWS, ROWS), F32)],
        compiler_params=params(),
        name="conv",
    )(got, *tables())


def grads_of(got_ref, fields_ref):
    conv = got_ref[pl.ds(0, CH, stride=2), :]
    grad_mixed = got_ref[pl.ds(1, CH, stride=2), :]
    fields = fields_ref[...].astype(F32)
    query, key = fields[0:CH], fields[CH : 2 * CH]
    value, grad = fields[2 * CH : 3 * CH], fields[3 * CH :]
    gated = query * conv
    return gated, jnp.concatenate([grad * conv, grad_mixed * value, grad_mixed * key], axis=0)


def parts_kernel(chan_ref, got_ref, fields_ref, w_ref, gated_ref, grads_ref, *out_refs):
    step = pl.program_id(0)

    @pl.when(step == 0)
    def _():
        gated, grads = grads_of(got_ref, fields_ref)
        gated_ref[...] = gated.T.astype(BF16)
        grads_ref[...] = grads.T.astype(BF16)

    part = nn_dot(grads_ref[...], w_ref[...]).astype(BF16)
    for slab, out_ref in enumerate(out_refs):

        @pl.when(step == slab)
        def _(out_ref=out_ref):
            out_ref[...] = part


def parts_call(got, fields, flat_w):
    chan = lax.axis_index("chan").reshape(1)
    slab = flat_w.shape[1] // 4
    whole = lambda shape: pl.BlockSpec(shape, lambda i, chan: (0, 0))
    return pl.pallas_call(
        parts_kernel,
        grid_spec=pltpu.PrefetchScalarGridSpec(
            num_scalar_prefetch=1,
            grid=(4,),
            in_specs=[
                whole((ROWS, ROWS)),
                whole((4 * CH, ROWS)),
                pl.BlockSpec((3 * CH, slab), lambda i, chan: (0, lax.rem(chan[0] + i + 1, 4))),
            ],
            out_specs=[whole((ROWS, CH)), whole((ROWS, 3 * CH))] + [whole((ROWS, slab))] * 4,
        ),
        out_shape=[
            jax.ShapeDtypeStruct((ROWS, CH), BF16),
            jax.ShapeDtypeStruct((ROWS, 3 * CH), BF16),
        ]
        + [jax.ShapeDtypeStruct((ROWS, slab), BF16)] * 4,
        compiler_params=params("arbitrary"),
        name="parts",
    )(chan, got, fields, flat_w)


def share_kernel(flip_ref, grads_ref, out_ref):
    out_ref[...] = nn_dot(flip_ref[...], grads_ref[...]).astype(BF16)


def share_call(flipped, grads):
    tile = 1024
    return pl.pallas_call(
        share_kernel,
        grid=(flipped.shape[0] // tile,),
        in_specs=[
            pl.BlockSpec((tile, ROWS), lambda i: (i, 0)),
            pl.BlockSpec((ROWS, 3 * CH), lambda i: (0, 0)),
        ],
        out_specs=pl.BlockSpec((tile, 3 * CH), lambda i: (i, 0)),
        out_shape=jax.ShapeDtypeStruct((flipped.shape[0], 3 * CH), BF16),
        compiler_params=params("arbitrary"),
        name="share",
    )(flipped, grads)


def reduce_over(value, axes, count):
    rows, cols = value.shape
    split = value.reshape(count, rows // count, cols)
    got = lax.all_to_all(split, axes, 0, 0, tiled=True)
    return jnp.sum(got.astype(F32), axis=0)


def shards(inputs, proj_weight, filters, out_grad):
    width = inputs.shape[1]
    flat_w = proj_weight.reshape(3 * CH, width)
    fields, send = fields_call(inputs, flat_w, filters, out_grad)
    got = lax.all_to_all(send.reshape(ROWS, 2, ROWS), SEQ, 0, 0, tiled=True)
    flipped = flip_call(inputs)
    conv = conv_call(got.reshape(2 * ROWS, ROWS))
    got = lax.all_to_all(conv.reshape(ROWS, 1, ROWS), SEQ, 0, 0, tiled=True)
    gated, grads, *parts = parts_call(got.reshape(ROWS, ROWS), fields, flat_w)
    arrived = [
        lax.ppermute(parts[k - 1], "chan", [(i, (i + k) % 4) for i in range(4)]) for k in (1, 2, 3)
    ]
    total = parts[3].astype(F32)
    for part in arrived:
        total = total + part.astype(F32)
    input_grad = total.astype(BF16)

    share = share_call(flipped, grads)
    share = reduce_over(share, ("core",), 2).astype(BF16)
    share = reduce_over(share, ("x", "y"), 16).astype(BF16)
    share = reduce_over(share, ("z",), 4)
    scale = 1.0 / math.sqrt(ROWS * ROWS)
    weight_grad = (share * scale).reshape(width // 128, 3, CH).astype(BF16)
    return (gated, weight_grad, input_grad)


def solution(mesh):
    split = Mesh(mesh.devices.reshape(4, 4, 4, 2, 4), SEQ + ("chan",))
    return jax.shard_map(
        shards,
        mesh=split,
        in_specs=(P(SEQ, None), P(None, "chan", None), P(SEQ, "chan"), P(SEQ, "chan")),
        out_specs=(P(SEQ, "chan"), P(SEQ, None, "chan"), P(SEQ, "chan")),
        check_vma=False,
    )
```

```python
import math

import jax
import jax.numpy as jnp
import numpy as np
from jax import lax
from jax.experimental import pallas as pl
from jax.experimental.pallas import tpu as pltpu
from jax.sharding import Mesh, PartitionSpec as P

F32 = jnp.float32
BF16 = jnp.bfloat16
SEQ = ("z", "x", "y", "core")
ROWS = 128
CH = 64
RING = 4
VMEM_LIMIT = 14 * 1024 * 1024
FIRST_LIMIT = 60 * 1024 * 1024


def params(*semantics, limit=VMEM_LIMIT):
    return pltpu.CompilerParams(
        vmem_limit_bytes=limit, dimension_semantics=semantics or None
    )


def nt_dot(left, right):
    return lax.dot_general(left, right, (((1,), (1,)), ((), ())), preferred_element_type=F32)


def tn_dot(left, right):
    return lax.dot_general(left, right, (((0,), (0,)), ((), ())), preferred_element_type=F32)


def nn_dot(left, right):
    return jnp.dot(left, right, preferred_element_type=F32)


def tables():
    length = ROWS * ROWS
    index = np.arange(ROWS)
    first = np.exp(-2j * np.pi * np.outer(index + 0.25, index) / ROWS)
    twist = np.exp(-2j * np.pi * np.outer(index + 0.25, index) / length)
    second = np.exp(-2j * np.pi * np.outer(index, index) / ROWS)
    first_rows = np.concatenate([first.real, first.imag], axis=0)
    second_fwd = np.block([[second.real, second.imag], [-second.imag, second.real]])
    second_bwd = np.block([[second.real, -second.imag], [second.imag, second.real]])
    first_bwd = np.concatenate([first.real.T, first.imag.T], axis=1) / length
    as_bf16 = lambda x: jnp.asarray(x, dtype=BF16)
    as_f32 = lambda x: jnp.asarray(x, dtype=F32)
    return (
        as_bf16(first_rows),
        as_f32(twist.real),
        as_f32(twist.imag),
        as_bf16(second_fwd),
        as_bf16(second_bwd),
        as_bf16(first_bwd),
    )


def fields_kernel(
    x_hbm, w_hbm, filt_hbm, grad_hbm, fields_ref, send_ref, x_ref, w_ref, filt_ref, grad_ref, scratch, sems
):
    parts, tile = x_ref.shape[0], x_ref.shape[2]
    small = [
        pltpu.make_async_copy(filt_hbm, filt_ref, sems.at[0]),
        pltpu.make_async_copy(grad_hbm, grad_ref, sems.at[1]),
    ]
    copies = []
    for part in range(parts):
        cols = slice(part * tile, (part + 1) * tile)
        copies.append(
            (
                pltpu.make_async_copy(x_hbm.at[:, cols], x_ref.at[part], sems.at[2 + 2 * part]),
                pltpu.make_async_copy(w_hbm.at[:, cols], w_ref.at[part], sems.at[3 + 2 * part]),
            )
        )
    for pair in copies:
        for copy in pair:
            copy.start()
    for copy in small:
        copy.start()
    acc = jnp.zeros((3 * CH, ROWS), F32)
    for part, pair in enumerate(copies):
        for copy in pair:
            copy.wait()
        acc += nt_dot(w_ref[part], x_ref[part])
    for copy in small:
        copy.wait()
    fields = acc.astype(BF16)
    grad_t = grad_ref[...]
    fields_ref[0 : 3 * CH, :] = fields
    fields_ref[3 * CH : 4 * CH, :] = grad_t
    query = fields[0:CH].astype(F32)
    key = fields[CH : 2 * CH].astype(F32)
    value = fields[2 * CH : 3 * CH].astype(F32)
    filt_t = filt_ref[...]
    scratch[pl.ds(0, CH, stride=4), :] = key * value
    scratch[pl.ds(1, CH, stride=4), :] = filt_t
    scratch[pl.ds(2, CH, stride=4), :] = grad_t.astype(F32) * query
    scratch[pl.ds(3, CH, stride=4), :] = filt_t
    send_ref[...] = scratch[...].astype(BF16)


def fields_call(inputs, flat_w, filters_t, grad_t):
    tile = 1024
    parts = inputs.shape[1] // tile
    return pl.pallas_call(
        fields_kernel,
        in_specs=[pl.BlockSpec(memory_space=pl.ANY)] * 4,
        out_shape=[jax.ShapeDtypeStruct((4 * CH, ROWS), BF16)] * 2,
        scratch_shapes=[
            pltpu.VMEM((parts, ROWS, tile), BF16),
            pltpu.VMEM((parts, 3 * CH, tile), BF16),
            pltpu.VMEM((CH, ROWS), F32),
            pltpu.VMEM((CH, ROWS), BF16),
            pltpu.VMEM((4 * CH, ROWS), F32),
            pltpu.SemaphoreType.DMA((2 + 2 * parts,)),
        ],
        compiler_params=params(limit=FIRST_LIMIT),
        name="fields",
    )(inputs, flat_w, filters_t, grad_t)


def flip_kernel(x_ref, other_ref, out_ref, scratch):
    core = lax.axis_index("core")
    for place, ref in enumerate((x_ref, other_ref)):
        scratch[...] = ref[...].astype(F32).T
        for block in range(out_ref.shape[0]):
            start = pl.multiple_of(64 * block + 32 * core, 32)
            rows = scratch[pl.ds(start, 32), :].astype(BF16)
            out_ref[block, 0, :, ROWS * place : ROWS * (place + 1)] = rows


def flip_call(inputs, other_inputs):
    tile = 1024
    steps = inputs.shape[1] // tile
    return pl.pallas_call(
        flip_kernel,
        grid=(steps,),
        in_specs=[pl.BlockSpec((ROWS, tile), lambda i: (0, i))] * 2,
        out_specs=pl.BlockSpec((tile // 64, 1, 32, 2 * ROWS), lambda i: (0, i, 0, 0)),
        out_shape=jax.ShapeDtypeStruct((tile // 64, steps, 32, 2 * ROWS), BF16),
        scratch_shapes=[pltpu.VMEM((tile, ROWS), F32)],
        compiler_params=params("arbitrary"),
        name="flip",
    )(inputs, other_inputs)


def conv_kernel(got_ref, e1_ref, twr_ref, twi_ref, e2_ref, e2b_ref, e1b_ref, out_ref, scratch, spread):
    sign = jnp.where(lax.axis_index("core") == 0, 1.0, -1.0).astype(F32)
    scratch[...] = got_ref[...].astype(F32)
    signal = scratch[pl.ds(0, ROWS, stride=2), :].astype(BF16)
    filt = scratch[pl.ds(1, ROWS, stride=2), :].astype(BF16)
    twr, twi = twr_ref[...], twi_ref[...]

    both = nn_dot(e1_ref[...], jnp.concatenate([signal, filt], axis=1))

    def twisted(part):
        re, im = part[0:ROWS], part[ROWS:]
        return jnp.concatenate([re * twr - im * twi, re * twi + im * twr], axis=1)

    mid = jnp.concatenate([twisted(both[:, 0:ROWS]), twisted(both[:, ROWS:])], axis=0)
    spec = nn_dot(mid.astype(BF16), e2_ref[...])
    sig_re, sig_im = spec[0:ROWS, 0:ROWS], spec[0:ROWS, ROWS:]
    fil_re, fil_im = spec[ROWS:, 0:ROWS], spec[ROWS:, ROWS:] * sign
    prod_re = sig_re * fil_re - sig_im * fil_im
    prod_im = sig_re * fil_im + sig_im * fil_re
    prod = jnp.concatenate([prod_re, prod_im], axis=1).astype(BF16)
    back = nn_dot(prod, e2b_ref[...])
    re, im = back[:, 0:ROWS], back[:, ROWS:]
    stack = jnp.concatenate([re * twr + im * twi, im * twr - re * twi], axis=0).astype(BF16)
    result = nn_dot(e1b_ref[...], stack)
    half = ROWS // 2
    spread[0:ROWS, :] = result
    even = spread[pl.ds(0, half, stride=2), :]
    odd = spread[pl.ds(1, half, stride=2), :]
    for place, rows in enumerate((even, odd, odd, even)):
        spread[pl.ds(place, half, stride=4), :] = rows
    out_ref[...] = spread[...].astype(BF16)


def conv_call(got):
    return pl.pallas_call(
        conv_kernel,
        out_shape=jax.ShapeDtypeStruct((2 * ROWS, ROWS), BF16),
        scratch_shapes=[pltpu.VMEM((2 * ROWS, ROWS), F32)] * 2,
        compiler_params=params(),
        name="conv",
    )(got, *tables())


def conv_of(scratch, block):
    conv = scratch[pl.ds(block, CH, stride=4), :]
    grad_mixed = scratch[pl.ds(2 + block, CH, stride=4), :]
    return conv, grad_mixed


def grads_of(conv, grad_mixed, fields):
    fields = fields.astype(F32)
    key, value = fields[CH : 2 * CH], fields[2 * CH : 3 * CH]
    grad = fields[3 * CH :]
    grads = jnp.concatenate([grad * conv, grad_mixed * value, grad_mixed * key], axis=0)
    return grads.T.astype(BF16)


def parts_kernel(chan_ref, got_ref, fields_ref, w_ref, gated_ref, grads_ref, *rest):
    part_refs, scratch = rest[:-1], rest[-1]

    @pl.when(pl.program_id(0) == 0)
    def _():
        scratch[...] = got_ref[...].astype(F32)
        conv, grad_mixed = conv_of(scratch, 0)
        fields = fields_ref[...]
        gated_ref[...] = (fields[0:CH].astype(F32) * conv).astype(BF16)
        grads_ref[...] = grads_of(conv, grad_mixed, fields)

    part = nn_dot(grads_ref[...], w_ref[...]).astype(BF16)
    for place, part_ref in enumerate(part_refs):

        @pl.when(pl.program_id(0) == place)
        def _(part_ref=part_ref):
            part_ref[...] = part


def parts_call(chan, got, fields, flat_w):
    slab = flat_w.shape[1] // RING
    whole = lambda shape: pl.BlockSpec(shape, lambda i, chan: (0, 0))
    shift = lambda i: jnp.where(i == 0, 2, jnp.where(i == 3, 0, 2 * i - 1))
    return pl.pallas_call(
        parts_kernel,
        grid_spec=pltpu.PrefetchScalarGridSpec(
            num_scalar_prefetch=1,
            grid=(RING,),
            in_specs=[
                whole((2 * ROWS, ROWS)),
                whole((4 * CH, ROWS)),
                pl.BlockSpec(
                    (3 * CH, slab), lambda i, chan: (0, lax.rem(chan[0] + shift(i), RING))
                ),
            ],
            out_specs=[whole((CH, ROWS)), whole((ROWS, 3 * CH))] + [whole((ROWS, slab))] * RING,
            scratch_shapes=[pltpu.VMEM((2 * ROWS, ROWS), F32)],
        ),
        out_shape=[
            jax.ShapeDtypeStruct((CH, ROWS), BF16),
            jax.ShapeDtypeStruct((ROWS, 3 * CH), BF16),
        ]
        + [jax.ShapeDtypeStruct((ROWS, slab), BF16)] * RING,
        compiler_params=params("arbitrary"),
        name="parts",
    )(chan, got, fields, flat_w)


def share_kernel(before_ref, got_ref, own_ref, other_ref, flipped_ref, out_ref, scratch, grads):
    del before_ref

    @pl.when(pl.program_id(0) == 0)
    def _():
        scratch[...] = got_ref[...].astype(F32)
        for block, ref in enumerate((own_ref, other_ref)):
            grads[ROWS * block : ROWS * (block + 1), :] = grads_of(
                *conv_of(scratch, block), ref[...]
            )

    blocks = flipped_ref.shape[0]
    total = nn_dot(flipped_ref[...].reshape(blocks * 32, 2 * ROWS), grads[...])
    out_ref[:, 0:32, :] = total[:, 0:ROWS].reshape(blocks, 32, ROWS).astype(BF16)
    last = total[:, ROWS:].reshape(blocks, 32, CH)
    out_ref[:, 32:48, :] = jnp.concatenate([last[:, 0:16], last[:, 16:32]], axis=2).astype(BF16)


def share_call(before, got, fields, other_fields, flipped):
    planes, steps = flipped.shape[:2]
    tile = 16
    whole = lambda shape: pl.BlockSpec(shape, lambda i: (0, 0))
    flipped = flipped.reshape(planes * steps, 32, 2 * ROWS)
    out = pl.pallas_call(
        share_kernel,
        grid=(planes * steps // tile,),
        in_specs=[
            pl.BlockSpec(memory_space=pl.ANY),
            whole((2 * ROWS, ROWS)),
            whole((4 * CH, ROWS)),
            whole((4 * CH, ROWS)),
            pl.BlockSpec((tile, 32, 2 * ROWS), lambda i: (i, 0, 0)),
        ],
        out_specs=pl.BlockSpec((tile, 48, ROWS), lambda i: (i, 0, 0)),
        out_shape=jax.ShapeDtypeStruct((planes * steps, 48, ROWS), BF16),
        scratch_shapes=[
            pltpu.VMEM((2 * ROWS, ROWS), F32),
            pltpu.VMEM((2 * ROWS, 3 * CH), BF16),
        ],
        compiler_params=params("arbitrary"),
        name="share",
    )(before, got, fields, other_fields, flipped)
    return out.reshape(planes, steps, 48, ROWS)


def stage_kernel(got_ref, out_ref):
    out_ref[...] = jnp.sum(got_ref[...].astype(F32), axis=0).astype(BF16)


def stage_call(got):
    return pl.pallas_call(
        stage_kernel,
        out_shape=jax.ShapeDtypeStruct(got.shape[1:], BF16),
        compiler_params=params(),
        name="stage",
    )(got)


def total_kernel(got_ref, out_ref):
    total = jnp.sum(got_ref[...].astype(F32), axis=0) * (1.0 / math.sqrt(ROWS * ROWS))
    total = total.astype(BF16)
    out_ref[0, :, :] = total[0:32, 0:CH]
    out_ref[1, :, :] = total[0:32, CH:]
    out_ref[2, 0:16, :] = total[32:48, 0:CH]
    out_ref[2, 16:32, :] = total[32:48, CH:]


def total_call(got):
    return pl.pallas_call(
        total_kernel,
        out_shape=jax.ShapeDtypeStruct((3, 32, CH), BF16),
        compiler_params=params(),
        name="total",
    )(got)


def turned(value, axis, shift):
    size = lax.axis_size(axis)
    return lax.ppermute(value, axis, [(i, (i + shift) % size) for i in range(size)])


def shards(inputs, proj_weight, filters, out_grad):
    width = inputs.shape[1]
    flat_w = proj_weight.reshape(3 * CH, width)
    chan = lax.axis_index("chan").reshape(1)
    fields, send = fields_call(inputs, flat_w, filters.T, out_grad.T)
    late_inputs, fields = lax.optimization_barrier((inputs, fields))
    other_inputs = turned(late_inputs, "core", 1)
    other_fields = turned(fields, "core", 1)
    got = lax.all_to_all(send.reshape(ROWS, 2, ROWS), SEQ, 0, 0, tiled=True)
    got, other_inputs, other_fields = lax.optimization_barrier((got, other_inputs, other_fields))
    flipped = flip_call(inputs, other_inputs)
    conv = conv_call(got.reshape(2 * ROWS, ROWS))
    got = lax.all_to_all(conv.reshape(ROWS, 2, ROWS), SEQ, 0, 0, tiled=True)
    got = got.reshape(2 * ROWS, ROWS)
    gated, grads, *parts = parts_call(chan, got, fields, flat_w)
    arrived = [turned(part, "chan", shift) for shift, part in zip((2, 1, 3), parts)]

    def weights(_, before):
        share = share_call(before, got, fields, other_fields, flipped)
        share = stage_call(lax.all_to_all(share, ("x", "y"), 0, 0, tiled=True))
        share = lax.all_to_all(share, "z", 0, 0, tiled=True)
        return total_call(share)

    once = jnp.minimum(lax.axis_index("x") + 1, 1)
    weight_grad = lax.fori_loop(0, once, weights, jnp.zeros((3, width // ROWS, CH), BF16))
    weight_grad, own = lax.optimization_barrier((weight_grad, parts[3]))
    weight_grad = jnp.transpose(weight_grad, (1, 0, 2))
    total = own.astype(F32)
    for part in arrived:
        total = total + part.astype(F32)
    input_grad = total.astype(BF16)
    return (gated.T, weight_grad, input_grad)


def solution(mesh):
    split = Mesh(mesh.devices.reshape(4, 4, 4, 2, 4), SEQ + ("chan",))
    return jax.shard_map(
        shards,
        mesh=split,
        in_specs=(P(SEQ, None), P(None, "chan", None), P(SEQ, "chan"), P(SEQ, "chan")),
        out_specs=(P(SEQ, "chan"), P(SEQ, None, "chan"), P(SEQ, "chan")),
        check_vma=False,
    )
```

```python
import math

import jax
import jax.numpy as jnp
import numpy as np
from jax import lax
from jax.experimental import pallas as pl
from jax.experimental.pallas import tpu as pltpu
from jax.sharding import Mesh, PartitionSpec as P

F32 = jnp.float32
BF16 = jnp.bfloat16
SEQ = ("z", "x", "y", "core")
ROWS = 128
CH = 64
RING = 4
VMEM_LIMIT = 14 * 1024 * 1024
FIRST_LIMIT = 60 * 1024 * 1024


def params(*semantics, limit=VMEM_LIMIT):
    return pltpu.CompilerParams(
        vmem_limit_bytes=limit, dimension_semantics=semantics or None
    )


def nt_dot(left, right):
    return lax.dot_general(left, right, (((1,), (1,)), ((), ())), preferred_element_type=F32)


def tn_dot(left, right):
    return lax.dot_general(left, right, (((0,), (0,)), ((), ())), preferred_element_type=F32)


def nn_dot(left, right):
    return jnp.dot(left, right, preferred_element_type=F32)


def tables():
    length = ROWS * ROWS
    index = np.arange(ROWS)
    first = np.exp(-2j * np.pi * np.outer(index + 0.25, index) / ROWS)
    twist = np.exp(-2j * np.pi * np.outer(index + 0.25, index) / length)
    second = np.exp(-2j * np.pi * np.outer(index, index) / ROWS)
    first_rows = np.concatenate([first.real, first.imag], axis=0)
    second_fwd = np.block([[second.real, second.imag], [-second.imag, second.real]])
    second_bwd = np.block([[second.real, -second.imag], [second.imag, second.real]])
    first_bwd = np.concatenate([first.real.T, first.imag.T], axis=1) / length
    as_bf16 = lambda x: jnp.asarray(x, dtype=BF16)
    as_f32 = lambda x: jnp.asarray(x, dtype=F32)
    return (
        as_bf16(first_rows),
        as_f32(twist.real),
        as_f32(twist.imag),
        as_bf16(second_fwd),
        as_bf16(second_bwd),
        as_bf16(first_bwd),
    )


def fields_kernel(
    x_hbm, w_hbm, filt_hbm, grad_hbm, fields_ref, send_ref, x_ref, w_ref, filt_ref, grad_ref, scratch, sems
):
    parts, tile = x_ref.shape[0], x_ref.shape[2]
    small = [
        pltpu.make_async_copy(filt_hbm, filt_ref, sems.at[0]),
        pltpu.make_async_copy(grad_hbm, grad_ref, sems.at[1]),
    ]
    copies = []
    for part in range(parts):
        cols = slice(part * tile, (part + 1) * tile)
        copies.append(
            (
                pltpu.make_async_copy(x_hbm.at[:, cols], x_ref.at[part], sems.at[2 + 2 * part]),
                pltpu.make_async_copy(w_hbm.at[:, cols], w_ref.at[part], sems.at[3 + 2 * part]),
            )
        )
    for pair in copies:
        for copy in pair:
            copy.start()
    for copy in small:
        copy.start()
    acc = jnp.zeros((3 * CH, ROWS), F32)
    for part, pair in enumerate(copies):
        for copy in pair:
            copy.wait()
        acc += nt_dot(w_ref[part], x_ref[part])
    for copy in small:
        copy.wait()
    fields = acc.astype(BF16)
    grad_t = grad_ref[...]
    fields_ref[0 : 3 * CH, :] = fields
    fields_ref[3 * CH : 4 * CH, :] = grad_t
    query = fields[0:CH].astype(F32)
    key = fields[CH : 2 * CH].astype(F32)
    value = fields[2 * CH : 3 * CH].astype(F32)
    filt_t = filt_ref[...]
    scratch[pl.ds(0, CH, stride=4), :] = key * value
    scratch[pl.ds(1, CH, stride=4), :] = filt_t
    scratch[pl.ds(2, CH, stride=4), :] = grad_t.astype(F32) * query
    scratch[pl.ds(3, CH, stride=4), :] = filt_t
    send_ref[...] = scratch[...].astype(BF16)


def fields_call(inputs, flat_w, filters_t, grad_t):
    tile = 1024
    parts = inputs.shape[1] // tile
    return pl.pallas_call(
        fields_kernel,
        in_specs=[pl.BlockSpec(memory_space=pl.ANY)] * 4,
        out_shape=[jax.ShapeDtypeStruct((4 * CH, ROWS), BF16)] * 2,
        scratch_shapes=[
            pltpu.VMEM((parts, ROWS, tile), BF16),
            pltpu.VMEM((parts, 3 * CH, tile), BF16),
            pltpu.VMEM((CH, ROWS), F32),
            pltpu.VMEM((CH, ROWS), BF16),
            pltpu.VMEM((4 * CH, ROWS), F32),
            pltpu.SemaphoreType.DMA((2 + 2 * parts,)),
        ],
        compiler_params=params(limit=FIRST_LIMIT),
        name="fields",
    )(inputs, flat_w, filters_t, grad_t)


def flip_kernel(x_ref, other_ref, out_ref, scratch):
    core = lax.axis_index("core")
    for place, ref in enumerate((x_ref, other_ref)):
        scratch[...] = ref[...].astype(F32).T
        for block in range(out_ref.shape[0]):
            start = pl.multiple_of(64 * block + 32 * core, 32)
            rows = scratch[pl.ds(start, 32), :].astype(BF16)
            out_ref[block, 0, :, ROWS * place : ROWS * (place + 1)] = rows


def flip_call(inputs, other_inputs):
    tile = 1024
    steps = inputs.shape[1] // tile
    return pl.pallas_call(
        flip_kernel,
        grid=(steps,),
        in_specs=[pl.BlockSpec((ROWS, tile), lambda i: (0, i))] * 2,
        out_specs=pl.BlockSpec((tile // 64, 1, 32, 2 * ROWS), lambda i: (0, i, 0, 0)),
        out_shape=jax.ShapeDtypeStruct((tile // 64, steps, 32, 2 * ROWS), BF16),
        scratch_shapes=[pltpu.VMEM((tile, ROWS), F32)],
        compiler_params=params("arbitrary"),
        name="flip",
    )(inputs, other_inputs)


def conv_kernel(got_ref, e1_ref, twr_ref, twi_ref, e2_ref, e2b_ref, e1b_ref, out_ref, scratch, spread):
    sign = jnp.where(lax.axis_index("core") == 0, 1.0, -1.0).astype(F32)
    scratch[...] = got_ref[...].astype(F32)
    signal = scratch[pl.ds(0, ROWS, stride=2), :].astype(BF16)
    filt = scratch[pl.ds(1, ROWS, stride=2), :].astype(BF16)
    twr, twi = twr_ref[...], twi_ref[...]

    both = nn_dot(e1_ref[...], jnp.concatenate([signal, filt], axis=1))

    def twisted(part):
        re, im = part[0:ROWS], part[ROWS:]
        return jnp.concatenate([re * twr - im * twi, re * twi + im * twr], axis=1)

    mid = jnp.concatenate([twisted(both[:, 0:ROWS]), twisted(both[:, ROWS:])], axis=0)
    spec = nn_dot(mid.astype(BF16), e2_ref[...])
    sig_re, sig_im = spec[0:ROWS, 0:ROWS], spec[0:ROWS, ROWS:]
    fil_re, fil_im = spec[ROWS:, 0:ROWS], spec[ROWS:, ROWS:] * sign
    prod_re = sig_re * fil_re - sig_im * fil_im
    prod_im = sig_re * fil_im + sig_im * fil_re
    prod = jnp.concatenate([prod_re, prod_im], axis=1).astype(BF16)
    back = nn_dot(prod, e2b_ref[...])
    re, im = back[:, 0:ROWS], back[:, ROWS:]
    stack = jnp.concatenate([re * twr + im * twi, im * twr - re * twi], axis=0).astype(BF16)
    result = nn_dot(e1b_ref[...], stack)
    half = ROWS // 2
    spread[0:ROWS, :] = result
    even = spread[pl.ds(0, half, stride=2), :]
    odd = spread[pl.ds(1, half, stride=2), :]
    for place, rows in enumerate((even, odd, odd, even)):
        spread[pl.ds(place, half, stride=4), :] = rows
    out_ref[...] = spread[...].astype(BF16)


def conv_call(got):
    return pl.pallas_call(
        conv_kernel,
        out_shape=jax.ShapeDtypeStruct((2 * ROWS, ROWS), BF16),
        scratch_shapes=[pltpu.VMEM((2 * ROWS, ROWS), F32)] * 2,
        compiler_params=params(),
        name="conv",
    )(got, *tables())


def conv_of(scratch, block):
    conv = scratch[pl.ds(block, CH, stride=4), :]
    grad_mixed = scratch[pl.ds(2 + block, CH, stride=4), :]
    return conv, grad_mixed


def grads_of(conv, grad_mixed, fields):
    fields = fields.astype(F32)
    key, value = fields[CH : 2 * CH], fields[2 * CH : 3 * CH]
    grad = fields[3 * CH :]
    grads = jnp.concatenate([grad * conv, grad_mixed * value, grad_mixed * key], axis=0)
    return grads.T.astype(BF16)


def parts_kernel(chan_ref, got_ref, fields_ref, w_ref, gated_ref, grads_ref, *rest):
    part_refs, scratch = rest[:-1], rest[-1]

    @pl.when(pl.program_id(0) == 0)
    def _():
        scratch[...] = got_ref[...].astype(F32)
        conv, grad_mixed = conv_of(scratch, 0)
        fields = fields_ref[...]
        gated_ref[...] = (fields[0:CH].astype(F32) * conv).astype(BF16)
        grads_ref[...] = grads_of(conv, grad_mixed, fields)

    part = nn_dot(grads_ref[...], w_ref[...]).astype(BF16)
    for place, part_ref in enumerate(part_refs):

        @pl.when(pl.program_id(0) == place)
        def _(part_ref=part_ref):
            part_ref[...] = part


def parts_call(chan, got, fields, flat_w):
    slab = flat_w.shape[1] // RING
    whole = lambda shape: pl.BlockSpec(shape, lambda i, chan: (0, 0))
    shift = lambda i: jnp.where(i == 0, 2, jnp.where(i == 3, 0, 2 * i - 1))
    return pl.pallas_call(
        parts_kernel,
        grid_spec=pltpu.PrefetchScalarGridSpec(
            num_scalar_prefetch=1,
            grid=(RING,),
            in_specs=[
                whole((2 * ROWS, ROWS)),
                whole((4 * CH, ROWS)),
                pl.BlockSpec(
                    (3 * CH, slab), lambda i, chan: (0, lax.rem(chan[0] + shift(i), RING))
                ),
            ],
            out_specs=[whole((CH, ROWS)), whole((ROWS, 3 * CH))] + [whole((ROWS, slab))] * RING,
            scratch_shapes=[pltpu.VMEM((2 * ROWS, ROWS), F32)],
        ),
        out_shape=[
            jax.ShapeDtypeStruct((CH, ROWS), BF16),
            jax.ShapeDtypeStruct((ROWS, 3 * CH), BF16),
        ]
        + [jax.ShapeDtypeStruct((ROWS, slab), BF16)] * RING,
        compiler_params=params("arbitrary"),
        name="parts",
    )(chan, got, fields, flat_w)


def last_kernel(own_ref, *refs):
    total = own_ref[...].astype(F32)
    for ref in refs[:-1]:
        total += ref[...].astype(F32)
    refs[-1][...] = total.astype(BF16)


def last_call(own, *others):
    return pl.pallas_call(
        last_kernel,
        out_shape=jax.ShapeDtypeStruct(own.shape, BF16),
        compiler_params=params(),
        name="last",
    )(own, *others)


def share_kernel(before_ref, got_ref, own_ref, other_ref, flipped_ref, out_ref, scratch, grads):
    del before_ref

    @pl.when(pl.program_id(0) == 0)
    def _():
        scratch[...] = got_ref[...].astype(F32)
        for block, ref in enumerate((own_ref, other_ref)):
            grads[ROWS * block : ROWS * (block + 1), :] = grads_of(
                *conv_of(scratch, block), ref[...]
            )

    blocks = flipped_ref.shape[0]
    total = nn_dot(flipped_ref[...].reshape(blocks * 32, 2 * ROWS), grads[...])
    out_ref[:, 0:32, :] = total[:, 0:ROWS].reshape(blocks, 32, ROWS).astype(BF16)
    last = total[:, ROWS:].reshape(blocks, 32, CH)
    out_ref[:, 32:48, :] = jnp.concatenate([last[:, 0:16], last[:, 16:32]], axis=2).astype(BF16)


def share_call(before, got, fields, other_fields, flipped):
    planes, steps = flipped.shape[:2]
    tile = 16
    whole = lambda shape: pl.BlockSpec(shape, lambda i: (0, 0))
    flipped = flipped.reshape(planes * steps, 32, 2 * ROWS)
    out = pl.pallas_call(
        share_kernel,
        grid=(planes * steps // tile,),
        in_specs=[
            pl.BlockSpec(memory_space=pl.ANY),
            whole((2 * ROWS, ROWS)),
            whole((4 * CH, ROWS)),
            whole((4 * CH, ROWS)),
            pl.BlockSpec((tile, 32, 2 * ROWS), lambda i: (i, 0, 0)),
        ],
        out_specs=pl.BlockSpec((tile, 48, ROWS), lambda i: (i, 0, 0)),
        out_shape=jax.ShapeDtypeStruct((planes * steps, 48, ROWS), BF16),
        scratch_shapes=[
            pltpu.VMEM((2 * ROWS, ROWS), F32),
            pltpu.VMEM((2 * ROWS, 3 * CH), BF16),
        ],
        compiler_params=params("arbitrary"),
        name="share",
    )(before, got, fields, other_fields, flipped)
    return out.reshape(planes, steps, 48, ROWS)


def stage_kernel(got_ref, out_ref):
    out_ref[...] = jnp.sum(got_ref[...].astype(F32), axis=0).astype(BF16)


def stage_call(got):
    return pl.pallas_call(
        stage_kernel,
        out_shape=jax.ShapeDtypeStruct(got.shape[1:], BF16),
        compiler_params=params(),
        name="stage",
    )(got)


def total_kernel(got_ref, out_ref):
    total = jnp.sum(got_ref[...].astype(F32), axis=0) * (1.0 / math.sqrt(ROWS * ROWS))
    total = total.astype(BF16)
    out_ref[0, :, :] = total[0:32, 0:CH]
    out_ref[1, :, :] = total[0:32, CH:]
    out_ref[2, 0:16, :] = total[32:48, 0:CH]
    out_ref[2, 16:32, :] = total[32:48, CH:]


def total_call(got):
    return pl.pallas_call(
        total_kernel,
        out_shape=jax.ShapeDtypeStruct((3, 32, CH), BF16),
        compiler_params=params(),
        name="total",
    )(got)


def turned(value, axis, shift):
    size = lax.axis_size(axis)
    return lax.ppermute(value, axis, [(i, (i + shift) % size) for i in range(size)])


def shards(inputs, proj_weight, filters, out_grad):
    width = inputs.shape[1]
    flat_w = proj_weight.reshape(3 * CH, width)
    chan = lax.axis_index("chan").reshape(1)
    fields, send = fields_call(inputs, flat_w, filters.T, out_grad.T)
    late_inputs, fields = lax.optimization_barrier((inputs, fields))
    other_inputs = turned(late_inputs, "core", 1)
    other_fields = turned(fields, "core", 1)
    got = lax.all_to_all(send.reshape(ROWS, 2, ROWS), SEQ, 0, 0, tiled=True)
    got, other_fields = lax.optimization_barrier((got, other_fields))
    conv = conv_call(got.reshape(2 * ROWS, ROWS))
    conv, other_inputs = lax.optimization_barrier((conv, other_inputs))
    flipped = flip_call(inputs, other_inputs)
    got = lax.all_to_all(conv.reshape(ROWS, 2, ROWS), SEQ, 0, 0, tiled=True)
    got, flipped = lax.optimization_barrier((got, flipped))
    got = got.reshape(2 * ROWS, ROWS)
    gated, grads, *parts = parts_call(chan, got, fields, flat_w)
    arrived = [turned(part, "chan", shift) for shift, part in zip((2, 1, 3), parts)]

    def weights(_, before):
        share = share_call(before, got, fields, other_fields, flipped)
        share = stage_call(lax.all_to_all(share, ("x", "y"), 0, 0, tiled=True))
        share = lax.all_to_all(share, "z", 0, 0, tiled=True)
        return total_call(share)

    once = jnp.minimum(lax.axis_index("x") + 1, 1)
    weight_grad = lax.fori_loop(0, once, weights, jnp.zeros((3, width // ROWS, CH), BF16))
    weight_grad, own = lax.optimization_barrier((weight_grad, parts[3]))
    weight_grad = jnp.transpose(weight_grad, (1, 0, 2))
    input_grad = last_call(own, *arrived)
    return (gated.T, weight_grad, input_grad)


def solution(mesh):
    split = Mesh(mesh.devices.reshape(4, 4, 4, 2, 4), SEQ + ("chan",))
    return jax.shard_map(
        shards,
        mesh=split,
        in_specs=(P(SEQ, None), P(None, "chan", None), P(SEQ, "chan"), P(SEQ, "chan")),
        out_specs=(P(SEQ, "chan"), P(SEQ, None, "chan"), P(SEQ, "chan")),
        check_vma=False,
    )
```

```python
import math

import jax
import jax.numpy as jnp
import numpy as np
from jax import lax
from jax.experimental import pallas as pl
from jax.experimental.pallas import tpu as pltpu
from jax.sharding import Mesh, PartitionSpec as P

F32 = jnp.float32
BF16 = jnp.bfloat16
SEQ = ("z", "x", "y", "core")
ROWS = 128
CH = 64
RING = 4
VMEM_LIMIT = 14 * 1024 * 1024
FIRST_LIMIT = 60 * 1024 * 1024


def params(*semantics, limit=VMEM_LIMIT):
    return pltpu.CompilerParams(
        vmem_limit_bytes=limit, dimension_semantics=semantics or None
    )


def nt_dot(left, right):
    return lax.dot_general(left, right, (((1,), (1,)), ((), ())), preferred_element_type=F32)


def tn_dot(left, right):
    return lax.dot_general(left, right, (((0,), (0,)), ((), ())), preferred_element_type=F32)


def nn_dot(left, right):
    return jnp.dot(left, right, preferred_element_type=F32)


def tables():
    length = ROWS * ROWS
    index = np.arange(ROWS)
    first = np.exp(-2j * np.pi * np.outer(index + 0.25, index) / ROWS)
    twist = np.exp(-2j * np.pi * np.outer(index + 0.25, index) / length)
    second = np.exp(-2j * np.pi * np.outer(index, index) / ROWS)
    first_rows = np.concatenate([first.real, first.imag], axis=0)
    second_fwd = np.block([[second.real, second.imag], [-second.imag, second.real]])
    second_bwd = np.block([[second.real, -second.imag], [second.imag, second.real]])
    first_bwd = np.concatenate([first.real.T, first.imag.T], axis=1) / length
    as_bf16 = lambda x: jnp.asarray(x, dtype=BF16)
    as_f32 = lambda x: jnp.asarray(x, dtype=F32)
    return (
        as_bf16(first_rows),
        as_f32(twist.real),
        as_f32(twist.imag),
        as_bf16(second_fwd),
        as_bf16(second_bwd),
        as_bf16(first_bwd),
    )


def fields_kernel(
    x_hbm, w_hbm, filt_hbm, grad_hbm, fields_ref, send_ref, x_ref, w_ref, filt_ref, grad_ref, scratch, sems
):
    parts, tile = x_ref.shape[0], x_ref.shape[2]
    small = [
        pltpu.make_async_copy(filt_hbm, filt_ref, sems.at[0]),
        pltpu.make_async_copy(grad_hbm, grad_ref, sems.at[1]),
    ]
    copies = []
    for part in range(parts):
        cols = slice(part * tile, (part + 1) * tile)
        copies.append(
            (
                pltpu.make_async_copy(x_hbm.at[:, cols], x_ref.at[part], sems.at[2 + 2 * part]),
                pltpu.make_async_copy(w_hbm.at[:, cols], w_ref.at[part], sems.at[3 + 2 * part]),
            )
        )
    for pair in copies:
        for copy in pair:
            copy.start()
    for copy in small:
        copy.start()
    acc = jnp.zeros((3 * CH, ROWS), F32)
    for part, pair in enumerate(copies):
        for copy in pair:
            copy.wait()
        acc += nt_dot(w_ref[part], x_ref[part])
    for copy in small:
        copy.wait()
    fields = acc.astype(BF16)
    grad_t = grad_ref[...]
    fields_ref[0 : 3 * CH, :] = fields
    fields_ref[3 * CH : 4 * CH, :] = grad_t
    query = fields[0:CH].astype(F32)
    key = fields[CH : 2 * CH].astype(F32)
    value = fields[2 * CH : 3 * CH].astype(F32)
    filt_t = filt_ref[...]
    scratch[pl.ds(0, CH, stride=4), :] = key * value
    scratch[pl.ds(1, CH, stride=4), :] = filt_t
    scratch[pl.ds(2, CH, stride=4), :] = grad_t.astype(F32) * query
    scratch[pl.ds(3, CH, stride=4), :] = filt_t
    send_ref[...] = scratch[...].astype(BF16)


def fields_call(inputs, flat_w, filters_t, grad_t):
    tile = 1024
    parts = inputs.shape[1] // tile
    return pl.pallas_call(
        fields_kernel,
        in_specs=[pl.BlockSpec(memory_space=pl.ANY)] * 4,
        out_shape=[jax.ShapeDtypeStruct((4 * CH, ROWS), BF16)] * 2,
        scratch_shapes=[
            pltpu.VMEM((parts, ROWS, tile), BF16),
            pltpu.VMEM((parts, 3 * CH, tile), BF16),
            pltpu.VMEM((CH, ROWS), F32),
            pltpu.VMEM((CH, ROWS), BF16),
            pltpu.VMEM((4 * CH, ROWS), F32),
            pltpu.SemaphoreType.DMA((2 + 2 * parts,)),
        ],
        compiler_params=params(limit=FIRST_LIMIT),
        name="fields",
    )(inputs, flat_w, filters_t, grad_t)


def flip_kernel(x_ref, other_ref, out_ref, scratch):
    core = lax.axis_index("core")
    for place, ref in enumerate((x_ref, other_ref)):
        scratch[...] = ref[...].astype(F32).T
        for block in range(out_ref.shape[0]):
            start = pl.multiple_of(64 * block + 32 * core, 32)
            rows = scratch[pl.ds(start, 32), :].astype(BF16)
            out_ref[block, 0, :, ROWS * place : ROWS * (place + 1)] = rows


def flip_call(inputs, other_inputs):
    tile = 1024
    steps = inputs.shape[1] // tile
    return pl.pallas_call(
        flip_kernel,
        grid=(steps,),
        in_specs=[pl.BlockSpec((ROWS, tile), lambda i: (0, i))] * 2,
        out_specs=pl.BlockSpec((tile // 64, 1, 32, 2 * ROWS), lambda i: (0, i, 0, 0)),
        out_shape=jax.ShapeDtypeStruct((tile // 64, steps, 32, 2 * ROWS), BF16),
        scratch_shapes=[pltpu.VMEM((tile, ROWS), F32)],
        compiler_params=params("arbitrary"),
        name="flip",
    )(inputs, other_inputs)


def conv_kernel(got_ref, e1_ref, twr_ref, twi_ref, e2_ref, e2b_ref, e1b_ref, out_ref, scratch, spread):
    sign = jnp.where(lax.axis_index("core") == 0, 1.0, -1.0).astype(F32)
    scratch[...] = got_ref[...].astype(F32)
    signal = scratch[pl.ds(0, ROWS, stride=2), :].astype(BF16)
    filt = scratch[pl.ds(1, ROWS, stride=2), :].astype(BF16)
    twr, twi = twr_ref[...], twi_ref[...]

    both = nn_dot(e1_ref[...], jnp.concatenate([signal, filt], axis=1))

    def twisted(part):
        re, im = part[0:ROWS], part[ROWS:]
        return jnp.concatenate([re * twr - im * twi, re * twi + im * twr], axis=1)

    mid = jnp.concatenate([twisted(both[:, 0:ROWS]), twisted(both[:, ROWS:])], axis=0)
    spec = nn_dot(mid.astype(BF16), e2_ref[...])
    sig_re, sig_im = spec[0:ROWS, 0:ROWS], spec[0:ROWS, ROWS:]
    fil_re, fil_im = spec[ROWS:, 0:ROWS], spec[ROWS:, ROWS:] * sign
    prod_re = sig_re * fil_re - sig_im * fil_im
    prod_im = sig_re * fil_im + sig_im * fil_re
    prod = jnp.concatenate([prod_re, prod_im], axis=1).astype(BF16)
    back = nn_dot(prod, e2b_ref[...])
    re, im = back[:, 0:ROWS], back[:, ROWS:]
    stack = jnp.concatenate([re * twr + im * twi, im * twr - re * twi], axis=0).astype(BF16)
    result = nn_dot(e1b_ref[...], stack)
    half = ROWS // 2
    spread[0:ROWS, :] = result
    even = spread[pl.ds(0, half, stride=2), :]
    odd = spread[pl.ds(1, half, stride=2), :]
    for place, rows in enumerate((even, odd, odd, even)):
        spread[pl.ds(place, half, stride=4), :] = rows
    out_ref[...] = spread[...].astype(BF16)


def conv_call(got):
    return pl.pallas_call(
        conv_kernel,
        out_shape=jax.ShapeDtypeStruct((2 * ROWS, ROWS), BF16),
        scratch_shapes=[pltpu.VMEM((2 * ROWS, ROWS), F32)] * 2,
        compiler_params=params(),
        name="conv",
    )(got, *tables())


def conv_of(scratch, block):
    conv = scratch[pl.ds(block, CH, stride=4), :]
    grad_mixed = scratch[pl.ds(2 + block, CH, stride=4), :]
    return conv, grad_mixed


def grads_of(conv, grad_mixed, fields):
    fields = fields.astype(F32)
    key, value = fields[CH : 2 * CH], fields[2 * CH : 3 * CH]
    grad = fields[3 * CH :]
    grads = jnp.concatenate([grad * conv, grad_mixed * value, grad_mixed * key], axis=0)
    return grads.T.astype(BF16)


def parts_kernel(chan_ref, got_ref, fields_ref, w_ref, gated_ref, grads_ref, *rest):
    part_refs, scratch = rest[:-1], rest[-1]

    @pl.when(pl.program_id(0) == 0)
    def _():
        scratch[...] = got_ref[...].astype(F32)
        conv, grad_mixed = conv_of(scratch, 0)
        fields = fields_ref[...]
        gated_ref[...] = (fields[0:CH].astype(F32) * conv).astype(BF16)
        grads_ref[...] = grads_of(conv, grad_mixed, fields)

    part = nn_dot(grads_ref[...], w_ref[...]).astype(BF16)
    for place, part_ref in enumerate(part_refs):

        @pl.when(pl.program_id(0) == place)
        def _(part_ref=part_ref):
            part_ref[...] = part


def parts_call(chan, got, fields, flat_w):
    slab = flat_w.shape[1] // RING
    whole = lambda shape: pl.BlockSpec(shape, lambda i, chan: (0, 0))
    shift = lambda i: jnp.where(i == 0, 2, jnp.where(i == 3, 0, 2 * i - 1))
    return pl.pallas_call(
        parts_kernel,
        grid_spec=pltpu.PrefetchScalarGridSpec(
            num_scalar_prefetch=1,
            grid=(RING,),
            in_specs=[
                whole((2 * ROWS, ROWS)),
                whole((4 * CH, ROWS)),
                pl.BlockSpec(
                    (3 * CH, slab), lambda i, chan: (0, lax.rem(chan[0] + shift(i), RING))
                ),
            ],
            out_specs=[whole((CH, ROWS)), whole((ROWS, 3 * CH))] + [whole((ROWS, slab))] * RING,
            scratch_shapes=[pltpu.VMEM((2 * ROWS, ROWS), F32)],
        ),
        out_shape=[
            jax.ShapeDtypeStruct((CH, ROWS), BF16),
            jax.ShapeDtypeStruct((ROWS, 3 * CH), BF16),
        ]
        + [jax.ShapeDtypeStruct((ROWS, slab), BF16)] * RING,
        compiler_params=params("arbitrary"),
        name="parts",
    )(chan, got, fields, flat_w)


def last_kernel(own_ref, *refs):
    total = own_ref[...].astype(F32)
    for ref in refs[:-1]:
        total += ref[...].astype(F32)
    refs[-1][...] = total.astype(BF16)


def last_call(own, *others):
    return pl.pallas_call(
        last_kernel,
        out_shape=jax.ShapeDtypeStruct(own.shape, BF16),
        compiler_params=params(),
        name="last",
    )(own, *others)


def share_kernel(before_ref, got_ref, own_ref, other_ref, flipped_ref, out_ref, scratch, grads):
    del before_ref

    @pl.when(pl.program_id(0) == 0)
    def _():
        scratch[...] = got_ref[...].astype(F32)
        for block, ref in enumerate((own_ref, other_ref)):
            grads[ROWS * block : ROWS * (block + 1), :] = grads_of(
                *conv_of(scratch, block), ref[...]
            )

    blocks = flipped_ref.shape[0]
    total = nn_dot(flipped_ref[...].reshape(blocks * 32, 2 * ROWS), grads[...])
    out_ref[:, 0:32, :] = total[:, 0:ROWS].reshape(blocks, 32, ROWS).astype(BF16)
    last = total[:, ROWS:].reshape(blocks, 32, CH)
    out_ref[:, 32:48, :] = jnp.concatenate([last[:, 0:16], last[:, 16:32]], axis=2).astype(BF16)


def share_call(before, got, fields, other_fields, flipped):
    planes, steps = flipped.shape[:2]
    tile = 16
    whole = lambda shape: pl.BlockSpec(shape, lambda i: (0, 0))
    flipped = flipped.reshape(planes * steps, 32, 2 * ROWS)
    out = pl.pallas_call(
        share_kernel,
        grid=(planes * steps // tile,),
        in_specs=[
            pl.BlockSpec(memory_space=pl.ANY),
            whole((2 * ROWS, ROWS)),
            whole((4 * CH, ROWS)),
            whole((4 * CH, ROWS)),
            pl.BlockSpec((tile, 32, 2 * ROWS), lambda i: (i, 0, 0)),
        ],
        out_specs=pl.BlockSpec((tile, 48, ROWS), lambda i: (i, 0, 0)),
        out_shape=jax.ShapeDtypeStruct((planes * steps, 48, ROWS), BF16),
        scratch_shapes=[
            pltpu.VMEM((2 * ROWS, ROWS), F32),
            pltpu.VMEM((2 * ROWS, 3 * CH), BF16),
        ],
        compiler_params=params("arbitrary"),
        name="share",
    )(before, got, fields, other_fields, flipped)
    return out.reshape(planes, steps, 48, ROWS)


def stage_kernel(got_ref, out_ref):
    out_ref[...] = jnp.sum(got_ref[...].astype(F32), axis=0).astype(BF16)


def stage_call(got):
    return pl.pallas_call(
        stage_kernel,
        out_shape=jax.ShapeDtypeStruct(got.shape[1:], BF16),
        compiler_params=params(),
        name="stage",
    )(got)


def total_kernel(got_ref, out_ref):
    total = jnp.sum(got_ref[...].astype(F32), axis=0) * (1.0 / math.sqrt(ROWS * ROWS))
    total = total.astype(BF16)
    out_ref[0, :, :] = total[0:32, 0:CH]
    out_ref[1, :, :] = total[0:32, CH:]
    out_ref[2, 0:16, :] = total[32:48, 0:CH]
    out_ref[2, 16:32, :] = total[32:48, CH:]


def total_call(got):
    return pl.pallas_call(
        total_kernel,
        out_shape=jax.ShapeDtypeStruct((3, 32, CH), BF16),
        compiler_params=params(),
        name="total",
    )(got)


def turned(value, axis, shift):
    size = lax.axis_size(axis)
    return lax.ppermute(value, axis, [(i, (i + shift) % size) for i in range(size)])


def shards(inputs, proj_weight, filters, out_grad):
    width = inputs.shape[1]
    flat_w = proj_weight.reshape(3 * CH, width)
    chan = lax.axis_index("chan").reshape(1)
    fields, send = fields_call(inputs, flat_w, filters.T, out_grad.T)
    late_inputs, fields = lax.optimization_barrier((inputs, fields))
    other_inputs = turned(late_inputs, "core", 1)
    other_fields = turned(fields, "core", 1)
    got = lax.all_to_all(send.reshape(ROWS, 2, ROWS), SEQ, 0, 0, tiled=True)
    got, other_inputs, other_fields = lax.optimization_barrier((got, other_inputs, other_fields))
    flipped = flip_call(inputs, other_inputs)
    conv = conv_call(got.reshape(2 * ROWS, ROWS))
    got = lax.all_to_all(conv.reshape(ROWS, 2, ROWS), SEQ, 0, 0, tiled=True)
    got = got.reshape(2 * ROWS, ROWS)
    gated, grads, *parts = parts_call(chan, got, fields, flat_w)
    arrived = [turned(part, "chan", shift) for shift, part in zip((2, 1, 3), parts)]

    def weights(_, before):
        share = share_call(before, got, fields, other_fields, flipped)
        share = stage_call(lax.all_to_all(share, ("x", "y"), 0, 0, tiled=True))
        share = lax.all_to_all(share, "z", 0, 0, tiled=True)
        return total_call(share)

    once = jnp.minimum(lax.axis_index("x") + 1, 1)
    weight_grad = lax.fori_loop(0, once, weights, jnp.zeros((3, width // ROWS, CH), BF16))
    weight_grad, own = lax.optimization_barrier((weight_grad, parts[3]))
    weight_grad = jnp.transpose(weight_grad, (1, 0, 2))
    input_grad = last_call(own, *arrived)
    return (gated.T, weight_grad, input_grad)


def solution(mesh):
    split = Mesh(mesh.devices.reshape(4, 4, 4, 2, 4), SEQ + ("chan",))
    return jax.shard_map(
        shards,
        mesh=split,
        in_specs=(P(SEQ, None), P(None, "chan", None), P(SEQ, "chan"), P(SEQ, "chan")),
        out_specs=(P(SEQ, "chan"), P(SEQ, None, "chan"), P(SEQ, "chan")),
        check_vma=False,
    )
```
